768 devices in a mesh: ship: 64 (over x, y, core), truck: 12 (over z).
Axes of the slice: x: 4, y: 8, z: 12, core: 2. Of those that a mesh axis runs over, the one named last changes fastest.
Arguments:
- tile_cost: bfloat16 [512, 12, 256, 256], P('ship', 'truck')
- warm_plan: bfloat16 [512, 12, 256, 256], P('ship', 'truck'), may hold values from 0 to 1, as said below
- slot_ship: int32 [512, 12], P('ship', 'truck'), may hold values from -1 to 23, as said below
- slot_truck: int32 [512, 12], P('ship', 'truck'), may hold values from 0 to 5
- ship_load: float32 [2, 393216], P(None, 'ship'), may hold values from 0.5 to 2
- truck_limit: float32 [2, 18432], P(None, 'truck'), may hold values from 4096 to 16384
- warm_ship_price: float32 [393216], P('ship'), may hold values from 0 to 1
- warm_truck_price: float32 [2, 18432], P(None, 'truck'), may hold values from 0 to 1
Outputs:
- final_plan: float32 [512, 12, 256, 256], P('ship', 'truck')
- ship_price: float32 [393216], P('ship')
- truck_price: float32 [2, 18432], P(None, 'truck')
- primal_weight: float32 [], replicated
The draws below stay inside these ranges and needn't reach their ends.
Inputs may be any that keep to these rules, and one draw needn't show every extreme that they name: `slot_ship`: on each device the live slots come first and name distinct blocks; at least 4 slots are live, and in every ship group one device has all 8 live. warm_plan is zero on empty slots.
All inputs are finite; a program needn't handle non-finite values.
Results may differ from the reference program's by a relative error of at most 0.0085.
Values sent between devices are 32-bit elements; how exact they have to be, the bound alone decides.
A program may use at most 32 MiB of HBM per device.

```python
import math
import jax
import jax.numpy as jnp
from jax import lax

TILE = 256
SHIPMENT_BLOCKS = 24
TB_DEV = 6
SLOT_LIMIT = 8
ITERS = 3
SHIPMENTS = 393216
TRUCKS = 18432
N_SHIP = 64
N_TRUCK = 12


def slot_block_list(key):
    folded = jax.random.fold_in(key, 11)
    count_key, order_key = jax.random.split(folded)
    count_values = jax.random.randint(count_key, (N_SHIP, N_TRUCK), SLOT_LIMIT // 2, SLOT_LIMIT + 1)
    ship_index = jnp.arange(N_SHIP)[:, None]
    truck_index = jnp.arange(N_TRUCK)[None, :]
    count_values = jnp.where(truck_index == ship_index % N_TRUCK, SLOT_LIMIT, count_values)
    scores = jax.random.randint(order_key, (N_SHIP, N_TRUCK, SHIPMENT_BLOCKS), 0, 1 << 20)
    scores = scores * SHIPMENT_BLOCKS + jnp.arange(SHIPMENT_BLOCKS)[None, None, :]
    rank_order = jnp.argsort(scores, axis=2)[:, :, :SLOT_LIMIT].astype(jnp.int32)
    active_flags = jnp.arange(SLOT_LIMIT)[None, None, :] < count_values[:, :, None]
    block_list = jnp.where(active_flags, rank_order, -1)
    return jnp.transpose(block_list, (0, 2, 1)).reshape(N_SHIP * SLOT_LIMIT, N_TRUCK).astype(jnp.int32)


def draw_slot_ship(key, part):
    return slot_block_list(key)


def draw_warm_plan(key, part):
    active_flags = (slot_block_list(key) >= 0).astype(jnp.float32)
    entry_values = jax.random.uniform(jax.random.fold_in(key, 12), (N_SHIP * SLOT_LIMIT, N_TRUCK, TILE, TILE))
    return (entry_values * active_flags[:, :, None, None]).astype(jnp.bfloat16)


def draw_tile_cost(key, part):
    full_shape = (N_SHIP * SLOT_LIMIT, N_TRUCK, TILE, TILE)
    key_list = jax.random.split(jax.random.fold_in(key, 13), 3)
    row_factor = jnp.exp(jax.random.uniform(key_list[1], (N_SHIP * SLOT_LIMIT, N_TRUCK, TILE, 1)) * math.log(10.0))
    column_factor = jnp.exp(jax.random.uniform(key_list[2], (N_SHIP * SLOT_LIMIT, N_TRUCK, 1, TILE)) * math.log(4.0))
    ship_group = (jnp.arange(N_SHIP * SLOT_LIMIT) // SLOT_LIMIT).astype(jnp.float32)
    rising = (1.0 + 2.0 * ship_group / max(N_SHIP - 1, 1)).reshape(-1, 1, 1, 1)
    normal_part = jax.random.normal(key_list[0], full_shape) - 0.2
    return (0.1 * normal_part * row_factor * column_factor * rising).astype(jnp.bfloat16)


def set_ends(values, rng, least, high):
    shape = values.shape
    place = [jax.random.randint(jax.random.fold_in(rng, axis), (), 0, shape[axis]) for axis in range(len(shape))]
    values = values.at[tuple(place)].set(least)
    longest = shape.index(max(shape))
    place[longest] = (place[longest] + 1) % shape[longest]
    return values.at[tuple(place)].set(high)


def block_scale(stream_key, extent, shards, low, largest):
    def one(position, shards_of):
        draws = jax.random.uniform(jax.random.fold_in(jax.random.fold_in(stream_key, 6), position), (shards_of,), jnp.float32, low / len(shards), largest / len(shards))
        return jnp.repeat(jnp.exp(draws), extent[position] // shards_of).reshape((-1,) + (1,) * (len(extent) - position - 1))

    level = one(*shards[0])
    for cut in shards[1:]:
        level = level * one(*cut)
    return level


def setup_inputs(seed: int = 0) -> dict:
    keys = jax.random.split(jax.random.key(seed), 9)
    tile_cost = draw_tile_cost(jax.random.fold_in(keys[8], 71), 0)
    warm_plan = draw_warm_plan(jax.random.fold_in(keys[8], 71), 0)
    slot_ship = draw_slot_ship(jax.random.fold_in(keys[8], 71), 0)
    slot_truck = set_ends(jax.random.randint(keys[3], (N_SHIP * SLOT_LIMIT, N_TRUCK), 0, TB_DEV), jax.random.fold_in(keys[3], 1), 0, TB_DEV - 1).astype(jnp.int32)
    ship_load = jnp.clip(jnp.exp(math.log(2.0) - 1.3862944 * jax.random.uniform(keys[4], (2, SHIPMENTS), jnp.float32) ** block_scale(keys[4], (2, SHIPMENTS), ((1, 64),), -0.2, 0.2)), 0.5, 2.0)
    truck_limit = jnp.clip(jnp.exp(math.log(16384.0) - 1.3862944 * jax.random.uniform(keys[5], (2, TRUCKS), jnp.float32) ** block_scale(keys[5], (2, TRUCKS), ((1, 12),), -0.2, 0.2)), 4096.0, 16384.0)
    warm_ship_price = jnp.clip(1.0 * jax.random.uniform(keys[6], (SHIPMENTS,), jnp.float32) ** block_scale(keys[6], (SHIPMENTS,), ((0, 64),), -0.2, 0.2), 0.0, 1.0)
    warm_truck_price = jnp.clip(1.0 * jax.random.uniform(keys[7], (2, TRUCKS), jnp.float32) ** block_scale(keys[7], (2, TRUCKS), ((1, 12),), -0.2, 0.2), 0.0, 1.0)
    return {"tile_cost": tile_cost, "warm_plan": warm_plan, "slot_ship": slot_ship, "slot_truck": slot_truck, "ship_load": ship_load, "truck_limit": truck_limit, "warm_ship_price": warm_ship_price, "warm_truck_price": warm_truck_price}


PRIMAL_DUAL_STEP = 0.5
EPSILON = 1e-06
HIGHEST_PRECISION = lax.Precision.HIGHEST

def reference(tile_cost, warm_plan, slot_ship, slot_truck, ship_load, truck_limit, warm_ship_price, warm_truck_price):
    row_scale = 1.0 / math.sqrt(TILE)
    cap_scale = 1.0 / math.sqrt(TILE * N_SHIP)
    cost_tiles = tile_cost.reshape(N_SHIP, SLOT_LIMIT, N_TRUCK, TILE, TILE)
    ship_slots = slot_ship.reshape(N_SHIP, SLOT_LIMIT, N_TRUCK)
    truck_slots = slot_truck.reshape(N_SHIP, SLOT_LIMIT, N_TRUCK)
    load_blocks = ship_load.reshape(2, N_SHIP, SHIPMENT_BLOCKS, TILE).transpose(1, 0, 2, 3)
    current_plan = warm_plan.astype(jnp.float32).reshape(N_SHIP, SLOT_LIMIT, N_TRUCK, TILE, TILE)
    price_ship = warm_ship_price.reshape(N_SHIP, SHIPMENT_BLOCKS, TILE)
    price_truck = warm_truck_price
    weight = jnp.float32(1.0)
    truck_column = jnp.arange(N_TRUCK, dtype=jnp.int32)[None, :]
    for iteration in range(ITERS):
        primal_update = PRIMAL_DUAL_STEP / weight
        dual_step = PRIMAL_DUAL_STEP * weight
        prices = price_truck.reshape(2, N_TRUCK, TB_DEV, TILE)

        def ship_group(group_items):
            cost_group, grouped_plan, shipment_group_index, truck_group_ids, load_group, price_group = group_items
            active_flags = shipment_group_index >= 0
            clamped_block = jnp.where(active_flags, shipment_group_index, 0)
            slot_price = price_group[clamped_block]
            slot_load = load_group[:, clamped_block]
            slot_cap = prices[:, truck_column, truck_group_ids]
            plan_gradient = cost_group.astype(jnp.float32) + row_scale * slot_price[..., :, None] + cap_scale * (slot_load[0][..., :, None] * slot_cap[0][..., None, :] + slot_load[1][..., :, None] * slot_cap[1][..., None, :])
            next_plan = jnp.clip(grouped_plan - primal_update * plan_gradient, 0.0, 1.0) * active_flags.astype(jnp.float32)[..., None, None]
            reflected = 2.0 * next_plan - grouped_plan
            row_numbers = jnp.where(active_flags, shipment_group_index, SHIPMENT_BLOCKS).reshape(-1)
            row_totals = jax.ops.segment_sum(lax.optimization_barrier(jnp.sum(reflected, axis=3)).reshape(-1, TILE), row_numbers, num_segments=SHIPMENT_BLOCKS + 1)[:SHIPMENT_BLOCKS]
            cap_slot = jnp.einsum('ckja,kjab->kjcb', slot_load, reflected, precision=HIGHEST_PRECISION)
            cap_ids = (truck_column * TB_DEV + truck_group_ids).reshape(-1)
            cap_totals = jax.ops.segment_sum(cap_slot.reshape(-1, 2, TILE), cap_ids, num_segments=N_TRUCK * TB_DEV)
            plan_moved = jnp.sum((next_plan - grouped_plan) ** 2)
            return (next_plan, row_totals, cap_totals, plan_moved)
        next_plan, row_totals, cap_totals, plan_moved = lax.map(ship_group, (cost_tiles, current_plan, ship_slots, truck_slots, load_blocks, price_ship))
        cap_whole = lax.optimization_barrier(jnp.sum(cap_totals, axis=0)).transpose(1, 0, 2).reshape(2, TRUCKS)
        new_ship = jnp.maximum(price_ship + dual_step * (row_scale * row_totals - row_scale), 0.0)
        new_truck = jnp.maximum(price_truck + dual_step * (cap_scale * cap_whole - cap_scale * truck_limit), 0.0)
        moved_plan = jnp.sum(plan_moved)
        moved_price = jnp.sum((new_ship - price_ship) ** 2) + jnp.sum((new_truck - price_truck) ** 2)
        weight = jnp.sqrt(weight * jnp.sqrt(moved_price + EPSILON) / jnp.sqrt(moved_plan + EPSILON))
        current_plan, price_ship, price_truck = (next_plan, new_ship, new_truck)
    return (current_plan.reshape(N_SHIP * SLOT_LIMIT, N_TRUCK, TILE, TILE), price_ship.reshape(SHIPMENTS), price_truck, weight)
```

```python
import functools
import math

import jax
import jax.numpy as jnp
from jax import lax
from jax.experimental import pallas as pl
from jax.experimental.pallas import tpu as pltpu
from jax.sharding import PartitionSpec as P

MESH = pl.DeviceIdType.MESH
ITERS = 3
STEP = 0.5
EPS = 1e-06
NX, NY, NC, NZ = 4, 8, 2, 12
SHIP = NX * NY * NC
OWNERS = NX * NC
SLOTS, TILE, SB, TB = 8, 256, 24, 6
HALF = TILE // 2
ROWS = 32
F32, BF16 = jnp.float32, jnp.bfloat16


def split(v):
    hi = v.astype(BF16).astype(F32)
    return hi, v - hi


def tree(parts):
    while len(parts) > 1:
        parts = [a + b for a, b in zip(parts[::2], parts[1::2])] + (
            [parts[-1]] if len(parts) % 2 else []
        )
    return parts[0]


def kernel(
    cost_hbm,
    warm_hbm,
    ss_ref,
    st_ref,
    load_ref,
    lim_ref,
    u_ref,
    p_ref,
    x_out,
    u_out,
    p_out,
    w_out,
    cost,
    warm,
    xs,
    gs,
    zh,
    zl,
    hh,
    hl,
    lb,
    at,
    oh,
    us,
    limtab,
    ptab,
    loadk,
    wv,
    sb_l,
    rb_l,
    sb_r,
    rb_r,
    sb_x,
    rb_x,
    sb_o,
    rb_o,
    sb_s,
    rb_s,
    sb_q,
    rb_q,
    in_sem,
    out_sem,
    send_sem,
    l_sem,
    r_sem,
    x_sem,
    o_sem,
    s_sem,
    q_sem,
    p_sem,
):
    i, j = lax.axis_index("ship"), lax.axis_index("truck")
    c = lax.rem(i, NC)
    y = lax.rem(lax.div(i, NC), NY)
    x = lax.div(i, NC * NY)
    own = x * NC + c
    row_scale = 1.0 / math.sqrt(TILE)
    cap_scale = 1.0 / math.sqrt(TILE * SHIP)

    loads_in = []
    for k in range(SLOTS):
        a = pltpu.make_async_copy(cost_hbm.at[k], cost.at[k], in_sem.at[0, k])
        b = pltpu.make_async_copy(warm_hbm.at[k], warm.at[k], in_sem.at[1, k])
        a.start()
        b.start()
        loads_in += [a, b]

    def place(ox, oy, oc):
        px, pc = lax.rem(x + ox, NX), lax.rem(c + oc, NC)
        return (px * NY + lax.rem(y + oy, NY)) * NC + pc, px * NC + pc

    cells = [(ox, oc) for ox in (2, 1, 3, 0) for oc in (1, 0)]

    def each_ship(act):
        def line(n, carry):
            half = (n + 1) // 2
            oy = jnp.where(n % 2 == 1, NY // 2 - half, NY // 2 + half)
            for ox, oc in cells:
                act(*place(ox, oy, oc))
            return carry

        lax.fori_loop(0, NY - 1, line, 0)
        for ox, oc in cells[:-1]:
            act(*place(ox, 0, oc))

    def z_at(n):
        half = (n + 1) // 2
        return lax.rem(j + jnp.where(n % 2 == 1, NZ // 2 - half, NZ // 2 + half), NZ)

    def each_truck(act):
        def line(n, carry):
            act(z_at(n))
            return carry

        lax.fori_loop(0, NZ - 1, line, 0)

    def each_owner(act):
        def line(n, carry):
            for ox, oc in cells:
                act(place(ox, 0, oc)[0], z_at(n))
            return carry

        lax.fori_loop(0, NZ - 1, line, 0)
        for ox, oc in cells[:-1]:
            act(place(ox, 0, oc)[0], j)

    barrier = pltpu.get_barrier_semaphore()

    def greet(di, dj):
        pl.semaphore_signal(barrier, inc=1, device_id=(di, dj), device_id_type=MESH)

    each_ship(lambda di, d: greet(di, j))

    def greet_line(n, carry):
        for ox, oc in cells:
            greet(place(ox, 0, oc)[0], z_at(n))
        return carry

    lax.fori_loop(0, NZ - 1, greet_line, 0)

    def send(src, dst, sem, kind, it, di, dj):
        pltpu.make_async_remote_copy(
            src_ref=src,
            dst_ref=dst,
            send_sem=send_sem.at[kind, it],
            recv_sem=sem,
            device_id=(di, dj),
            device_id_type=MESH,
        ).start()

    def wait(buf, sem):
        pltpu.make_async_copy(buf, buf, sem).wait()

    ship_of = jnp.broadcast_to(ss_ref[...], (SLOTS, TILE))
    truck_of = jnp.broadcast_to(st_ref[...], (SLOTS, TILE))
    sub = lax.broadcasted_iota(jnp.int32, (SLOTS, TILE), 0)
    for h in range(2):
        us[:, h * HALF : (h + 1) * HALF] = u_ref[pl.ds(h, SB, stride=2), :]
    for d in range(OWNERS):
        g, h = d // 2, d % 2
        for r in range(3):
            col = ((g % 2) * 3 + r) * TILE + h * HALF
            limtab[d, r : r + 1, :] = lim_ref[g // 2 : g // 2 + 1, col : col + HALF]
            ptab[0, d, r : r + 1, :] = p_ref[g // 2 : g // 2 + 1, col : col + HALF]
    for n in range(2):
        acc = jnp.zeros((SLOTS, TILE), F32)
        for s in range(SB):
            acc = jnp.where(
                ship_of == s, load_ref[n : n + 1, s * TILE : (s + 1) * TILE], acc
            )
        loadk[n] = acc
    for k in range(SLOTS):
        truck_k = jnp.broadcast_to(st_ref[k : k + 1, :], (SLOTS, TILE))
        hi, lo = [], []
        for g in range(4):
            v = jnp.broadcast_to(loadk[g // 2, k : k + 1, :], (SLOTS, TILE))
            v = jnp.where((sub < 3) & (truck_k == sub + 3 * (g % 2)), v, 0.0)
            a, b = split(v)
            hi.append(a)
            lo.append(b)
        lb[k] = jnp.concatenate(hi + lo, axis=0).astype(BF16)
    sb_o[...] = jnp.broadcast_to(ss_ref[...], (SLOTS, HALF)).astype(F32)
    rb_o[j] = sb_o[...]
    one_row = lax.broadcasted_iota(jnp.int32, (16, HALF), 0)

    def prices_u():
        u8 = jnp.zeros((SLOTS, TILE), F32)
        for s in range(SB):
            u8 = jnp.where(ship_of == s, us[s : s + 1, :], u8)
        u_hi, u_lo = split(u8)
        a_hi, a_lo = split(loadk[0])
        b_hi, b_lo = split(loadk[1])
        stack = [u_hi, u_lo, a_hi, a_lo, a_hi, b_hi, b_lo, b_hi]
        stack.append(jnp.zeros((128 - 8 * len(stack), TILE), F32))
        at[...] = jnp.transpose(jnp.concatenate(stack, axis=0)).astype(BF16)

    def gradient(it):
        parts = []
        for n in range(2):
            p8 = []
            for h in range(2):
                acc = jnp.zeros((SLOTS, HALF), F32)
                for t in range(TB):
                    d = (2 * n + t // 3) * 2 + h
                    acc = jnp.where(
                        truck_of[:, :HALF] == t, ptab[it, d, t % 3 : t % 3 + 1, :], acc
                    )
                p8.append(acc)
            p_hi, p_lo = split(jnp.concatenate(p8, axis=1) * cap_scale)
            parts += [p_hi, p_hi, p_lo]
        ones = jnp.full((SLOTS, TILE), row_scale, F32)
        parts = [ones, ones] + parts
        for k in range(SLOTS):
            rows = [jnp.where(sub == k, v, 0.0) for v in parts]
            rows.append(jnp.zeros((128 - 8 * len(rows), TILE), F32))
            b_k = jnp.concatenate(rows, axis=0).astype(BF16)
            live = jnp.broadcast_to(ss_ref[k : k + 1, :], (HALF, TILE)) >= 0
            for a in range(0, TILE, HALF):
                v = jnp.dot(at[a : a + HALF, :], b_k, preferred_element_type=F32)
                v = v + cost[k, a : a + HALF, :].astype(F32)
                gs[k, a : a + HALF, :] = jnp.where(live, v, 0.0)

    wv[...] = jnp.ones_like(wv)
    prices_u()
    for copy in loads_in:
        copy.wait()
    for k in range(SLOTS):
        xs[k] = warm[k].astype(F32)
    gradient(0)

    pl.semaphore_wait(barrier, SHIP - 1 + (NZ - 1) * OWNERS)
    each_truck(lambda dj: send(sb_o, rb_o.at[j], o_sem.at[0], 4, 0, i, dj))

    def iteration(it, carry):
        weight = wv[...]
        tau = STEP / weight
        sigma = STEP * weight
        moved = jnp.zeros((8, HALF), F32)
        cap_hi = jnp.zeros((64, TILE), F32)
        cap_lo = jnp.zeros((32, TILE), F32)
        rows_acc = jnp.zeros((16, TILE), F32)
        tau_b = jnp.broadcast_to(tau[0:1, 0:1], (ROWS, TILE))
        for k in range(SLOTS):
            for a in range(0, TILE, ROWS):
                old = xs[k, a : a + ROWS, :]
                new = jnp.clip(old - tau_b * gs[k, a : a + ROWS, :], 0.0, 1.0)
                xs[k, a : a + ROWS, :] = new
                step = new - old
                z = new + step
                z_hi = z.astype(BF16)
                zh[k, a : a + ROWS, :] = z_hi
                zl[k, a : a + ROWS, :] = (z - z_hi.astype(F32)).astype(BF16)
                zs = z[:, :HALF] + z[:, HALF:]
                s_hi = zs.astype(BF16)
                hh[k, a : a + ROWS, :] = s_hi
                hl[k, a : a + ROWS, :] = (zs - s_hi.astype(F32)).astype(BF16)
                sq = step * step
                sq = sq[:, :HALF] + sq[:, HALF:]
                moved = moved + jnp.sum(sq.reshape(ROWS // 8, 8, HALF), axis=0)
            cap_hi = cap_hi + jnp.dot(lb[k], zh[k], preferred_element_type=F32)
            cap_lo = cap_lo + jnp.dot(lb[k, :32, :], zl[k], preferred_element_type=F32)
        cap = cap_hi[:32] + cap_hi[32:] + cap_lo
        for d in range(OWNERS):
            g, h = d // 2, d % 2
            sb_l[it, d] = cap[8 * g : 8 * g + 3, h * HALF : (h + 1) * HALF]
        rb_l[it, i] = sb_l[it, own]
        each_ship(
            lambda di, d: send(
                sb_l.at[it, d], rb_l.at[it, i], l_sem.at[it], 0, it, di, j
            )
        )

        nt = (((1,), (1,)), ((), ()))
        for k in range(SLOTS):
            pick = jnp.where(one_row == k, 1.0, 0.0).astype(BF16)
            rows_acc = rows_acc + lax.dot_general(
                pick, hh[k], nt, preferred_element_type=F32
            )
            rows_acc = rows_acc + lax.dot_general(
                pick, hl[k], nt, preferred_element_type=F32
            )
        sb_r[it] = rows_acc[:SLOTS]
        rb_r[it, j] = rows_acc[:SLOTS]
        each_truck(
            lambda dj: send(
                sb_r.at[it], rb_r.at[it, j], r_sem.at[it], 1, it, i, dj
            )
        )
        moved = jnp.sum(moved, axis=0, keepdims=True)
        sb_x[it] = moved
        rb_x[it, j] = moved
        each_truck(
            lambda dj: send(
                sb_x.at[it], rb_x.at[it, j], x_sem.at[it], 2, it, i, dj
            )
        )

        @pl.when(it == ITERS - 1)
        def _():
            pltpu.make_async_copy(xs, x_out, out_sem.at[0]).start()

        wait(rb_l.at[it, pl.ds(0, SHIP - 1)], l_sem.at[it])
        total = tree([rb_l[it, s] for s in range(SHIP)])
        old_p = ptab[it, own]
        sig3 = jnp.broadcast_to(sigma[0:1, 0:1], (3, HALF))
        new_p = jnp.maximum(
            old_p + sig3 * (cap_scale * total - cap_scale * limtab[own]), 0.0
        )
        ptab[it + 1, own] = new_p
        step_p = jnp.sum((new_p - old_p) ** 2, axis=0, keepdims=True)
        sb_s[it] = step_p
        rb_s[it, own * NZ + j] = step_p
        each_owner(
            lambda di, dj: send(
                sb_s.at[it], rb_s.at[it, own * NZ + j], s_sem.at[it], 3, it, di, dj
            )
        )
        for ox, oc in cells[:-1]:
            send(
                ptab.at[it + 1, own],
                ptab.at[it + 1, own],
                p_sem.at[it],
                5,
                it,
                place(ox, 0, oc)[0],
                j,
            )

        @pl.when(it == 0)
        def _():
            wait(rb_o.at[pl.ds(0, NZ - 1)], o_sem.at[0])
            lane = lax.broadcasted_iota(jnp.int32, (NZ * SLOTS, HALF), 1).astype(F32)
            hot = jnp.where(rb_o[...].reshape(NZ * SLOTS, HALF) == lane, 1.0, 0.0)
            hot = jnp.concatenate(
                [hot, jnp.zeros((128 - NZ * SLOTS, HALF), F32)], axis=0
            )
            oh[...] = jnp.transpose(hot)[:32].astype(BF16)

        wait(rb_r.at[it, pl.ds(0, NZ - 1)], r_sem.at[it])
        wait(rb_x.at[it, pl.ds(0, NZ - 1)], x_sem.at[it])
        parts = rb_r[it].reshape(NZ * SLOTS, TILE)
        parts = jnp.concatenate(
            [parts, jnp.zeros((128 - NZ * SLOTS, TILE), F32)], axis=0
        )
        p_hi, p_lo = split(parts)
        rows = jnp.dot(oh[...], p_hi.astype(BF16), preferred_element_type=F32)
        rows = rows + jnp.dot(oh[...], p_lo.astype(BF16), preferred_element_type=F32)
        rows = rows[:SB]
        old_u = us[...]
        sig24 = jnp.broadcast_to(sigma[0:1, 0:1], (SB, TILE))
        new_u = jnp.maximum(old_u + sig24 * (row_scale * rows - row_scale), 0.0)
        us[...] = new_u
        step_u = (new_u - old_u) ** 2
        step_u = jnp.sum(step_u[:, :HALF] + step_u[:, HALF:], axis=0, keepdims=True)
        step_x = tree([rb_x[it, n] for n in range(NZ)])
        step_u = step_u + pltpu.roll(step_u, HALF // 2, 1)
        step_x = step_x + pltpu.roll(step_x, HALF // 2, 1)
        low = lax.broadcasted_iota(jnp.int32, (1, HALF), 1) < HALF // 2
        both = jnp.where(low, step_x, step_u)
        sb_q[it] = both
        rb_q[it, i] = both
        each_ship(
            lambda di, d: send(
                sb_q.at[it], rb_q.at[it, i], q_sem.at[it], 6, it, di, j
            )
        )

        prices_u()
        wait(ptab.at[it + 1, pl.ds(0, OWNERS - 1)], p_sem.at[it])
        gradient(it + 1)
        wait(rb_q.at[it, pl.ds(0, SHIP - 1)], q_sem.at[it])
        q_sum = tree([rb_q[it, s] for s in range(SHIP)])
        wait(rb_s.at[it, pl.ds(0, OWNERS * NZ - 1)], s_sem.at[it])
        s_sum = tree([rb_s[it, s] for s in range(OWNERS * NZ)])
        dx = jnp.sum(jnp.where(low, q_sum, 0.0), axis=1, keepdims=True)
        dy = jnp.sum(jnp.where(low, 0.0, q_sum) + s_sum, axis=1, keepdims=True)
        weight = jnp.sqrt(
            weight[0:1, :]
            * jnp.sqrt(jnp.broadcast_to(dy, (1, HALF)) + EPS)
            / jnp.sqrt(jnp.broadcast_to(dx, (1, HALF)) + EPS)
        )
        wv[...] = jnp.broadcast_to(weight, wv.shape)
        return carry

    lax.fori_loop(0, ITERS, iteration, 0)

    for h in range(2):
        u_out[pl.ds(h, SB, stride=2), :] = us[:, h * HALF : (h + 1) * HALF]
    for d in range(OWNERS):
        g, h = d // 2, d % 2
        for r in range(3):
            col = ((g % 2) * 3 + r) * TILE + h * HALF
            p_out[g // 2 : g // 2 + 1, col : col + HALF] = ptab[ITERS, d, r : r + 1, :]
    w_out[...] = wv[0:1, :]
    for it in range(ITERS):
        wait(rb_l.at[it, pl.ds(0, SHIP - 1)], send_sem.at[0, it])
        wait(rb_r.at[it, pl.ds(0, NZ - 1)], send_sem.at[1, it])
        wait(rb_x.at[it, pl.ds(0, NZ - 1)], send_sem.at[2, it])
        wait(rb_s.at[it, pl.ds(0, OWNERS * NZ - 1)], send_sem.at[3, it])
        wait(ptab.at[it + 1, pl.ds(0, OWNERS - 1)], send_sem.at[5, it])
        wait(rb_q.at[it, pl.ds(0, SHIP - 1)], send_sem.at[6, it])
    wait(rb_o.at[pl.ds(0, NZ - 1)], send_sem.at[4, 0])
    pltpu.make_async_copy(xs, x_out, out_sem.at[0]).wait()


def on_device(cost, warm, slot_ship, slot_truck, load, limit, ship_price, truck_price):
    vmem, hbm = (
        pl.BlockSpec(memory_space=pltpu.VMEM),
        pl.BlockSpec(memory_space=pl.ANY),
    )
    dma = pltpu.SemaphoreType.DMA
    plan, prices, caps, weight = pl.pallas_call(
        kernel,
        out_shape=(
            jax.ShapeDtypeStruct((SLOTS, TILE, TILE), F32),
            jax.ShapeDtypeStruct((2 * SB, HALF), F32),
            jax.ShapeDtypeStruct(truck_price.shape, F32),
            jax.ShapeDtypeStruct((1, HALF), F32),
        ),
        in_specs=[hbm, hbm, vmem, vmem, vmem, vmem, vmem, vmem],
        out_specs=(hbm, vmem, vmem, vmem),
        scratch_shapes=[
            pltpu.VMEM((SLOTS, TILE, TILE), BF16),
            pltpu.VMEM((SLOTS, TILE, TILE), BF16),
            pltpu.VMEM((SLOTS, TILE, TILE), F32),
            pltpu.VMEM((SLOTS, TILE, TILE), F32),
            pltpu.VMEM((SLOTS, TILE, TILE), BF16),
            pltpu.VMEM((SLOTS, TILE, TILE), BF16),
            pltpu.VMEM((SLOTS, TILE, HALF), BF16),
            pltpu.VMEM((SLOTS, TILE, HALF), BF16),
            pltpu.VMEM((SLOTS, 64, TILE), BF16),
            pltpu.VMEM((TILE, 128), BF16),
            pltpu.VMEM((32, 128), BF16),
            pltpu.VMEM((SB, TILE), F32),
            pltpu.VMEM((OWNERS, 3, HALF), F32),
            pltpu.VMEM((ITERS + 1, OWNERS, 3, HALF), F32),
            pltpu.VMEM((2, SLOTS, TILE), F32),
            pltpu.VMEM((8, HALF), F32),
            pltpu.VMEM((ITERS, OWNERS, 3, HALF), F32),
            pltpu.VMEM((ITERS, SHIP, 3, HALF), F32),
            pltpu.VMEM((ITERS, SLOTS, TILE), F32),
            pltpu.VMEM((ITERS, NZ, SLOTS, TILE), F32),
            pltpu.VMEM((ITERS, 1, HALF), F32),
            pltpu.VMEM((ITERS, NZ, 1, HALF), F32),
            pltpu.VMEM((SLOTS, HALF), F32),
            pltpu.VMEM((NZ, SLOTS, HALF), F32),
            pltpu.VMEM((ITERS, 1, HALF), F32),
            pltpu.VMEM((ITERS, OWNERS * NZ, 1, HALF), F32),
            pltpu.VMEM((ITERS, 1, HALF), F32),
            pltpu.VMEM((ITERS, SHIP, 1, HALF), F32),
            dma((2, SLOTS)),
            dma((1,)),
            dma((7, ITERS)),
            dma((ITERS,)),
            dma((ITERS,)),
            dma((ITERS,)),
            dma((1,)),
            dma((ITERS,)),
            dma((ITERS,)),
            dma((ITERS,)),
        ],
        compiler_params=pltpu.CompilerParams(
            collective_id=0, has_side_effects=True, vmem_limit_bytes=40 << 20
        ),
    )(
        cost.reshape(SLOTS, TILE, TILE),
        warm.reshape(SLOTS, TILE, TILE),
        slot_ship,
        slot_truck,
        load,
        limit,
        ship_price.reshape(2 * SB, HALF),
        truck_price,
    )
    return (
        plan.reshape(SLOTS, 1, TILE, TILE),
        prices.reshape(-1),
        caps,
        weight[0, 0],
    )


def solution(mesh):
    in_specs = (
        P("ship", "truck", None, None),
        P("ship", "truck", None, None),
        P("ship", "truck"),
        P("ship", "truck"),
        P(None, "ship"),
        P(None, "truck"),
        P("ship"),
        P(None, "truck"),
    )
    out_specs = (P("ship", "truck", None, None), P("ship"), P(None, "truck"), P())
    return jax.shard_map(
        on_device, mesh=mesh, in_specs=in_specs, out_specs=out_specs, check_vma=False
    )
```

```python
import functools
import math

import jax
import jax.numpy as jnp
from jax import lax
from jax.experimental import pallas as pl
from jax.experimental.pallas import tpu as pltpu
from jax.sharding import PartitionSpec as P

MESH = pl.DeviceIdType.MESH
ITERS = 3
STEP = 0.5
EPS = 1e-06
NX, NY, NC, NZ = 4, 8, 2, 12
SHIP = NX * NY * NC
OWNERS = NX * NC
SLOTS, TILE, SB, TB = 8, 256, 24, 6
HALF = TILE // 2
ROWS = 32
F32, BF16 = jnp.float32, jnp.bfloat16


def split(v):
    hi = v.astype(BF16).astype(F32)
    return hi, v - hi


def tree(parts):
    while len(parts) > 1:
        parts = [a + b for a, b in zip(parts[::2], parts[1::2])] + (
            [parts[-1]] if len(parts) % 2 else []
        )
    return parts[0]


def kernel(
    cost_hbm,
    warm_hbm,
    ss_hbm,
    st_hbm,
    load_hbm,
    lim_hbm,
    u_hbm,
    p_hbm,
    x_out,
    u_out,
    p_out,
    w_out,
    cost,
    warm,
    xs,
    ss_row,
    st_row,
    load_ref,
    lim_ref,
    u_ref,
    p_ref,
    gs,
    zh,
    zl,
    hh,
    hl,
    lb,
    at,
    oh,
    us,
    limtab,
    ptab,
    loadk,
    slot_of,
    wv,
    sb_l,
    rb_l,
    sb_r,
    rb_r,
    sb_x,
    rb_x,
    sb_o,
    rb_o,
    sb_s,
    rb_s,
    sb_q,
    rb_q,
    in_sem,
    out_sem,
    send_sem,
    l_sem,
    r_sem,
    x_sem,
    o_sem,
    s_sem,
    q_sem,
    p_sem,
):
    i, j = lax.axis_index("ship"), lax.axis_index("truck")
    c = lax.rem(i, NC)
    y = lax.rem(lax.div(i, NC), NY)
    x = lax.div(i, NC * NY)
    own = lax.rem(x + 2 * lax.rem(y, 2), NX) * NC + c
    row_scale = 1.0 / math.sqrt(TILE)
    cap_scale = 1.0 / math.sqrt(TILE * SHIP)

    def place(ox, oy, oc):
        px, py, pc = lax.rem(x + ox, NX), lax.rem(y + oy, NY), lax.rem(c + oc, NC)
        piece = lax.rem(px + 2 * lax.rem(py, 2), NX) * NC + pc
        return (px * NY + py) * NC + pc, piece

    cells = [(ox, oc) for ox in (2, 1, 3, 0) for oc in (1, 0)]
    takers = [
        (ox, oy, oc) for ox, oy in ((1, 0), (3, 0), (0, NY - 1), (0, 0)) for oc in (1, 0)
    ]

    def each_ship(act):
        def line(n, carry):
            half = (n + 1) // 2
            oy = jnp.where(n % 2 == 1, NY // 2 - half, NY // 2 + half)
            for ox, oc in cells:
                act(*place(ox, oy, oc))
            return carry

        lax.fori_loop(0, NY - 1, line, 0)
        for ox, oc in cells[:-1]:
            act(*place(ox, 0, oc))

    def z_at(n):
        half = (n + 1) // 2
        return lax.rem(j + jnp.where(n % 2 == 1, NZ // 2 - half, NZ // 2 + half), NZ)

    def each_truck(act):
        def line(n, carry):
            act(z_at(n))
            return carry

        lax.fori_loop(0, NZ - 1, line, 0)

    def each_taker(act):
        def line(n, carry):
            for at_offset in takers:
                act(place(*at_offset)[0], z_at(n))
            return carry

        lax.fori_loop(0, NZ - 1, line, 0)
        for at_offset in takers[:-1]:
            act(place(*at_offset)[0], j)

    barrier = pltpu.get_barrier_semaphore()

    def greet(di, dj):
        pl.semaphore_signal(barrier, inc=1, device_id=(di, dj), device_id_type=MESH)

    each_truck(lambda dj: greet(i, dj))
    each_ship(lambda di, d: greet(di, j))

    loads_in = [
        pltpu.make_async_copy(src, dst, in_sem.at[2, n])
        for n, (src, dst) in enumerate(
            (
                (ss_hbm, ss_row),
                (st_hbm, st_row),
                (load_hbm, load_ref),
                (lim_hbm, lim_ref),
                (u_hbm, u_ref),
                (p_hbm, p_ref),
            )
        )
    ]
    tiles_in = []
    for k in range(SLOTS):
        tiles_in += [
            pltpu.make_async_copy(warm_hbm.at[k], warm.at[k], in_sem.at[1, k]),
            pltpu.make_async_copy(cost_hbm.at[k], cost.at[k], in_sem.at[0, k]),
        ]
    for copy in loads_in + tiles_in:
        copy.start()

    def send(src, dst, sem, kind, it, di, dj):
        pltpu.make_async_remote_copy(
            src_ref=src,
            dst_ref=dst,
            send_sem=send_sem.at[kind, it],
            recv_sem=sem,
            device_id=(di, dj),
            device_id_type=MESH,
        ).start()

    def wait(buf, sem):
        pltpu.make_async_copy(buf, buf, sem).wait()

    for copy in loads_in:
        copy.wait()
    square = (SLOTS, SLOTS)
    diagonal = lax.broadcasted_iota(jnp.int32, square, 0) == lax.broadcasted_iota(
        jnp.int32, square, 1
    )

    def column(row):
        v = jnp.broadcast_to(row[...].astype(F32), square)
        return jnp.sum(jnp.where(diagonal, v, 0.0), axis=1, keepdims=True)

    ship_f = jnp.broadcast_to(column(ss_row), (SLOTS, TILE))
    ship_of = ship_f.astype(jnp.int32)
    truck_of = jnp.broadcast_to(column(st_row), (SLOTS, TILE)).astype(jnp.int32)
    slot_of[0] = ship_of
    slot_of[1] = truck_of
    sub = lax.broadcasted_iota(jnp.int32, (SLOTS, TILE), 0)
    for h in range(2):
        us[:, h * HALF : (h + 1) * HALF] = u_ref[pl.ds(h, SB, stride=2), :]
    for d in range(OWNERS):
        g, h = d // 2, d % 2
        for r in range(3):
            col = ((g % 2) * 3 + r) * TILE + h * HALF
            limtab[d, r : r + 1, :] = lim_ref[g // 2 : g // 2 + 1, col : col + HALF]
            ptab[0, d, r : r + 1, :] = p_ref[g // 2 : g // 2 + 1, col : col + HALF]
    for n in range(2):
        acc = jnp.zeros((SLOTS, TILE), F32)
        for s in range(SB):
            acc = jnp.where(
                ship_of == s, load_ref[n : n + 1, s * TILE : (s + 1) * TILE], acc
            )
        loadk[n] = acc
    for k in range(SLOTS):
        truck_k = jnp.broadcast_to(slot_of[1, k : k + 1, :], (SLOTS, TILE))
        hi, lo = [], []
        for g in range(4):
            v = jnp.broadcast_to(loadk[g // 2, k : k + 1, :], (SLOTS, TILE))
            v = jnp.where((sub < 3) & (truck_k == sub + 3 * (g % 2)), v, 0.0)
            a, b = split(v)
            hi.append(a)
            lo.append(b)
        lb[k] = jnp.concatenate(hi + lo, axis=0).astype(BF16)
    sb_o[...] = ship_f[:, :HALF]
    rb_o[j] = sb_o[...]
    one_row = lax.broadcasted_iota(jnp.int32, (16, HALF), 0)

    def prices_u():
        u8 = jnp.zeros((SLOTS, TILE), F32)
        for s in range(SB):
            u8 = jnp.where(ship_of == s, us[s : s + 1, :], u8)
        u_hi, u_lo = split(u8)
        a_hi, a_lo = split(loadk[0])
        b_hi, b_lo = split(loadk[1])
        stack = [u_hi, u_lo, a_hi, a_lo, a_hi, b_hi, b_lo, b_hi]
        stack.append(jnp.zeros((128 - 8 * len(stack), TILE), F32))
        at[...] = jnp.transpose(jnp.concatenate(stack, axis=0)).astype(BF16)

    def gradient(it):
        parts = []
        for n in range(2):
            p8 = []
            for h in range(2):
                acc = jnp.zeros((SLOTS, HALF), F32)
                for t in range(TB):
                    d = (2 * n + t // 3) * 2 + h
                    acc = jnp.where(
                        truck_of[:, :HALF] == t, ptab[it, d, t % 3 : t % 3 + 1, :], acc
                    )
                p8.append(acc)
            p_hi, p_lo = split(jnp.concatenate(p8, axis=1) * cap_scale)
            parts += [p_hi, p_hi, p_lo]
        ones = jnp.full((SLOTS, TILE), row_scale, F32)
        parts = [ones, ones] + parts
        for k in range(SLOTS):
            rows = [jnp.where(sub == k, v, 0.0) for v in parts]
            rows.append(jnp.zeros((128 - 8 * len(rows), TILE), F32))
            b_k = jnp.concatenate(rows, axis=0).astype(BF16)
            live = jnp.broadcast_to(slot_of[0, k : k + 1, :], (HALF, TILE)) >= 0
            for a in range(0, TILE, HALF):
                v = jnp.dot(at[a : a + HALF, :], b_k, preferred_element_type=F32)
                v = v + cost[k, a : a + HALF, :].astype(F32)
                gs[k, a : a + HALF, :] = jnp.where(live, v, 0.0)

    wv[...] = jnp.ones_like(wv)
    prices_u()
    for copy in tiles_in:
        copy.wait()
    for k in range(SLOTS):
        xs[k] = warm[k].astype(F32)
    gradient(0)

    pl.semaphore_wait(barrier, SHIP - 1 + NZ - 1)
    each_truck(lambda dj: send(sb_o, rb_o.at[j], o_sem.at[0], 4, 0, i, dj))

    def iteration(it, carry):
        weight = wv[...]
        tau = STEP / weight
        sigma = STEP * weight
        moved = jnp.zeros((8, HALF), F32)
        cap_hi = jnp.zeros((64, TILE), F32)
        cap_lo = jnp.zeros((32, TILE), F32)
        rows_acc = jnp.zeros((16, TILE), F32)
        nt = (((1,), (1,)), ((), ()))
        tau_b = jnp.broadcast_to(tau[0:1, 0:1], (ROWS, TILE))
        for k in range(SLOTS):
            for a in range(0, TILE, ROWS):
                old = xs[k, a : a + ROWS, :]
                new = jnp.clip(old - tau_b * gs[k, a : a + ROWS, :], 0.0, 1.0)
                xs[k, a : a + ROWS, :] = new
                step = new - old
                z = new + step
                z_hi = z.astype(BF16)
                zh[k, a : a + ROWS, :] = z_hi
                zl[k, a : a + ROWS, :] = (z - z_hi.astype(F32)).astype(BF16)
                zs = z[:, :HALF] + z[:, HALF:]
                s_hi = zs.astype(BF16)
                hh[k, a : a + ROWS, :] = s_hi
                hl[k, a : a + ROWS, :] = (zs - s_hi.astype(F32)).astype(BF16)
                sq = step * step
                sq = sq[:, :HALF] + sq[:, HALF:]
                moved = moved + jnp.sum(sq.reshape(ROWS // 8, 8, HALF), axis=0)
            pick = jnp.where(one_row == k, 1.0, 0.0).astype(BF16)
            for v in (hh, hl):
                rows_acc = rows_acc + lax.dot_general(
                    pick, v[k], nt, preferred_element_type=F32
                )
            cap_hi = cap_hi + jnp.dot(lb[k], zh[k], preferred_element_type=F32)
            cap_lo = cap_lo + jnp.dot(lb[k, :32, :], zl[k], preferred_element_type=F32)
        sb_r[it] = rows_acc[:SLOTS]
        rb_r[it, j] = rows_acc[:SLOTS]
        each_truck(
            lambda dj: send(
                sb_r.at[it], rb_r.at[it, j], r_sem.at[it], 1, it, i, dj
            )
        )
        cap = cap_hi[:32] + cap_hi[32:] + cap_lo
        for d in range(OWNERS):
            g, h = d // 2, d % 2
            sb_l[it, d] = cap[8 * g : 8 * g + 3, h * HALF : (h + 1) * HALF]
        rb_l[it, i] = sb_l[it, own]
        each_ship(
            lambda di, d: send(
                sb_l.at[it, d], rb_l.at[it, i], l_sem.at[it], 0, it, di, j
            )
        )
        moved = jnp.sum(moved, axis=0, keepdims=True)
        sb_x[it] = moved
        rb_x[it, pl.ds(j, 1)] = moved
        each_truck(
            lambda dj: send(
                sb_x.at[it], rb_x.at[it, pl.ds(j, 1)], x_sem.at[it], 2, it, i, dj
            )
        )

        @pl.when(it == ITERS - 1)
        def _():
            pltpu.make_async_copy(xs, x_out, out_sem.at[0]).start()

        wait(rb_l.at[it, pl.ds(0, SHIP - 1)], l_sem.at[it])
        total = tree([rb_l[it, s] for s in range(SHIP)])
        old_p = ptab[it, own]
        sig3 = jnp.broadcast_to(sigma[0:1, 0:1], (3, HALF))
        new_p = jnp.maximum(
            old_p + sig3 * (cap_scale * total - cap_scale * limtab[own]), 0.0
        )
        ptab[it + 1, own] = new_p
        step_p = jnp.sum((new_p - old_p) ** 2, axis=0, keepdims=True)
        sb_s[it] = step_p
        rb_s[it, pl.ds(own * NZ + j, 1)] = step_p
        each_taker(
            lambda di, dj: send(
                sb_s.at[it], rb_s.at[it, pl.ds(own * NZ + j, 1)], s_sem.at[it], 3, it, di, dj
            )
        )
        for at_offset in takers[:-1]:
            send(
                ptab.at[it + 1, own],
                ptab.at[it + 1, own],
                p_sem.at[it],
                5,
                it,
                place(*at_offset)[0],
                j,
            )

        @pl.when(it == 0)
        def _():
            wait(rb_o.at[pl.ds(0, NZ - 1)], o_sem.at[0])
            lane = lax.broadcasted_iota(jnp.int32, (NZ * SLOTS, HALF), 1).astype(F32)
            hot = jnp.where(rb_o[...].reshape(NZ * SLOTS, HALF) == lane, 1.0, 0.0)
            hot = jnp.concatenate(
                [hot, jnp.zeros((128 - NZ * SLOTS, HALF), F32)], axis=0
            )
            oh[...] = jnp.transpose(hot)[:32].astype(BF16)

        wait(rb_r.at[it, pl.ds(0, NZ - 1)], r_sem.at[it])
        wait(rb_x.at[it, pl.ds(0, NZ - 1)], x_sem.at[it])
        parts = rb_r[it].reshape(NZ * SLOTS, TILE)
        parts = jnp.concatenate(
            [parts, jnp.zeros((128 - NZ * SLOTS, TILE), F32)], axis=0
        )
        p_hi, p_lo = split(parts)
        rows = jnp.dot(oh[...], p_hi.astype(BF16), preferred_element_type=F32)
        rows = rows + jnp.dot(oh[...], p_lo.astype(BF16), preferred_element_type=F32)
        rows = rows[:SB]
        old_u = us[...]
        sig24 = jnp.broadcast_to(sigma[0:1, 0:1], (SB, TILE))
        new_u = jnp.maximum(old_u + sig24 * (row_scale * rows - row_scale), 0.0)
        us[...] = new_u
        step_u = (new_u - old_u) ** 2
        step_u = jnp.sum(step_u[:, :HALF] + step_u[:, HALF:], axis=0, keepdims=True)
        step_x = jnp.sum(rb_x[it], axis=0, keepdims=True)
        step_u = step_u + pltpu.roll(step_u, HALF // 2, 1)
        step_x = step_x + pltpu.roll(step_x, HALF // 2, 1)
        low = lax.broadcasted_iota(jnp.int32, (1, HALF), 1) < HALF // 2
        both = jnp.where(low, step_x, step_u)
        sb_q[it] = both
        rb_q[it, pl.ds(i, 1)] = both
        each_ship(
            lambda di, d: send(
                sb_q.at[it], rb_q.at[it, pl.ds(i, 1)], q_sem.at[it], 6, it, di, j
            )
        )

        prices_u()
        wait(ptab.at[it + 1, pl.ds(0, OWNERS - 1)], p_sem.at[it])
        gradient(it + 1)
        wait(rb_q.at[it, pl.ds(0, SHIP - 1)], q_sem.at[it])
        q_sum = jnp.sum(rb_q[it], axis=0, keepdims=True)
        wait(rb_s.at[it, pl.ds(0, OWNERS * NZ - 1)], s_sem.at[it])
        s_sum = jnp.sum(rb_s[it], axis=0, keepdims=True)
        dx = jnp.sum(jnp.where(low, q_sum, 0.0), axis=1, keepdims=True)
        dy = jnp.sum(jnp.where(low, 0.0, q_sum) + s_sum, axis=1, keepdims=True)
        weight = jnp.sqrt(
            weight[0:1, :]
            * jnp.sqrt(jnp.broadcast_to(dy, (1, HALF)) + EPS)
            / jnp.sqrt(jnp.broadcast_to(dx, (1, HALF)) + EPS)
        )
        wv[...] = jnp.broadcast_to(weight, wv.shape)
        return carry

    lax.fori_loop(0, ITERS, iteration, 0)

    for h in range(2):
        u_out[pl.ds(h, SB, stride=2), :] = us[:, h * HALF : (h + 1) * HALF]
    for d in range(OWNERS):
        g, h = d // 2, d % 2
        for r in range(3):
            col = ((g % 2) * 3 + r) * TILE + h * HALF
            p_out[g // 2 : g // 2 + 1, col : col + HALF] = ptab[ITERS, d, r : r + 1, :]
    w_out[...] = wv[0:1, :]
    for it in range(ITERS):
        wait(rb_l.at[it, pl.ds(0, SHIP - 1)], send_sem.at[0, it])
        wait(rb_r.at[it, pl.ds(0, NZ - 1)], send_sem.at[1, it])
        wait(rb_x.at[it, pl.ds(0, NZ - 1)], send_sem.at[2, it])
        wait(rb_s.at[it, pl.ds(0, OWNERS * NZ - 1)], send_sem.at[3, it])
        wait(ptab.at[it + 1, pl.ds(0, OWNERS - 1)], send_sem.at[5, it])
        wait(rb_q.at[it, pl.ds(0, SHIP - 1)], send_sem.at[6, it])
    wait(rb_o.at[pl.ds(0, NZ - 1)], send_sem.at[4, 0])
    pltpu.make_async_copy(xs, x_out, out_sem.at[0]).wait()


def copy_out(*refs):
    ins, outs, held, in_sem, out_sem = refs[:4], refs[4:8], refs[8:12], *refs[12:]
    pairs = [(ins[0].at[k], held[0].at[k], outs[0].at[k]) for k in range(SLOTS)]
    pairs += list(zip(ins[1:], held[1:], outs[1:]))
    first = [
        pltpu.make_async_copy(a, b, in_sem.at[n]) for n, (a, b, _) in enumerate(pairs)
    ]
    second = [
        pltpu.make_async_copy(b, c, out_sem.at[n]) for n, (_, b, c) in enumerate(pairs)
    ]
    for copy in first:
        copy.start()
    for a, b in zip(first, second):
        a.wait()
        b.start()
    for copy in second:
        copy.wait()


def on_device(cost, warm, slot_ship, slot_truck, load, limit, ship_price, truck_price):
    vmem, hbm = (
        pl.BlockSpec(memory_space=pltpu.VMEM),
        pl.BlockSpec(memory_space=pltpu.HBM),
    )
    dma = pltpu.SemaphoreType.DMA
    plan, prices, caps, weight = pl.pallas_call(
        kernel,
        out_shape=(
            jax.ShapeDtypeStruct((SLOTS, TILE, TILE), F32),
            jax.ShapeDtypeStruct((2 * SB, HALF), F32),
            jax.ShapeDtypeStruct(truck_price.shape, F32),
            jax.ShapeDtypeStruct((1, HALF), F32),
        ),
        in_specs=[hbm] * 8,
        out_specs=(hbm, vmem, vmem, vmem),
        scratch_shapes=[
            pltpu.VMEM((SLOTS, TILE, TILE), BF16),
            pltpu.VMEM((SLOTS, TILE, TILE), BF16),
            pltpu.VMEM((SLOTS, TILE, TILE), F32),
            pltpu.VMEM((1, SLOTS), jnp.int32),
            pltpu.VMEM((1, SLOTS), jnp.int32),
            pltpu.VMEM(load.shape, F32),
            pltpu.VMEM(limit.shape, F32),
            pltpu.VMEM((2 * SB, HALF), F32),
            pltpu.VMEM(truck_price.shape, F32),
            pltpu.VMEM((SLOTS, TILE, TILE), F32),
            pltpu.VMEM((SLOTS, TILE, TILE), BF16),
            pltpu.VMEM((SLOTS, TILE, TILE), BF16),
            pltpu.VMEM((SLOTS, TILE, HALF), BF16),
            pltpu.VMEM((SLOTS, TILE, HALF), BF16),
            pltpu.VMEM((SLOTS, 64, TILE), BF16),
            pltpu.VMEM((TILE, 128), BF16),
            pltpu.VMEM((32, 128), BF16),
            pltpu.VMEM((SB, TILE), F32),
            pltpu.VMEM((OWNERS, 3, HALF), F32),
            pltpu.VMEM((ITERS + 1, OWNERS, 3, HALF), F32),
            pltpu.VMEM((2, SLOTS, TILE), F32),
            pltpu.VMEM((2, SLOTS, TILE), jnp.int32),
            pltpu.VMEM((8, HALF), F32),
            pltpu.VMEM((ITERS, OWNERS, 3, HALF), F32),
            pltpu.VMEM((ITERS, SHIP, 3, HALF), F32),
            pltpu.VMEM((ITERS, SLOTS, TILE), F32),
            pltpu.VMEM((ITERS, NZ, SLOTS, TILE), F32),
            pltpu.VMEM((ITERS, 1, HALF), F32),
            pltpu.VMEM((ITERS, NZ, HALF), F32),
            pltpu.VMEM((SLOTS, HALF), F32),
            pltpu.VMEM((NZ, SLOTS, HALF), F32),
            pltpu.VMEM((ITERS, 1, HALF), F32),
            pltpu.VMEM((ITERS, OWNERS * NZ, HALF), F32),
            pltpu.VMEM((ITERS, 1, HALF), F32),
            pltpu.VMEM((ITERS, SHIP, HALF), F32),
            dma((3, SLOTS)),
            dma((1,)),
            dma((7, ITERS)),
            dma((ITERS,)),
            dma((ITERS,)),
            dma((ITERS,)),
            dma((1,)),
            dma((ITERS,)),
            dma((ITERS,)),
            dma((ITERS,)),
        ],
        compiler_params=pltpu.CompilerParams(
            collective_id=0, has_side_effects=True, vmem_limit_bytes=60 << 20
        ),
    )(
        cost.reshape(SLOTS, TILE, TILE),
        warm.reshape(SLOTS, TILE, TILE),
        slot_ship.reshape(1, SLOTS),
        slot_truck.reshape(1, SLOTS),
        load,
        limit,
        ship_price.reshape(2 * SB, HALF),
        truck_price,
    )
    results = (plan, prices, caps, weight)
    plan, prices, caps, weight = pl.pallas_call(
        copy_out,
        out_shape=[jax.ShapeDtypeStruct(v.shape, v.dtype) for v in results],
        in_specs=[hbm] * 4,
        out_specs=[hbm] * 4,
        scratch_shapes=[pltpu.VMEM(v.shape, v.dtype) for v in results]
        + [dma((SLOTS + 3,)), dma((SLOTS + 3,))],
    )(*results)
    return (
        plan.reshape(SLOTS, 1, TILE, TILE),
        prices.reshape(-1),
        caps,
        weight[0, 0],
    )


def solution(mesh):
    in_specs = (
        P("ship", "truck", None, None),
        P("ship", "truck", None, None),
        P("ship", "truck"),
        P("ship", "truck"),
        P(None, "ship"),
        P(None, "truck"),
        P("ship"),
        P(None, "truck"),
    )
    out_specs = (P("ship", "truck", None, None), P("ship"), P(None, "truck"), P())
    return jax.shard_map(
        on_device, mesh=mesh, in_specs=in_specs, out_specs=out_specs, check_vma=False
    )
```

```python
import functools
import math

import jax
import jax.numpy as jnp
from jax import lax
from jax.experimental import pallas as pl
from jax.experimental.pallas import tpu as pltpu
from jax.sharding import PartitionSpec as P

MESH = pl.DeviceIdType.MESH
ITERS = 3
STEP = 0.5
EPS = 1e-06
NX, NY, NC, NZ = 4, 8, 2, 12
SHIP = NX * NY * NC
OWNERS = NX * NC
SLOTS, TILE, SB, TB = 8, 256, 24, 6
HALF = TILE // 2
ROWS = 16
F32, BF16 = jnp.float32, jnp.bfloat16


def split(v):
    hi = v.astype(BF16).astype(F32)
    return hi, v - hi


def tree(parts):
    while len(parts) > 1:
        parts = [a + b for a, b in zip(parts[::2], parts[1::2])] + (
            [parts[-1]] if len(parts) % 2 else []
        )
    return parts[0]


def kernel(
    cost_hbm,
    warm_hbm,
    ss_hbm,
    st_hbm,
    load_hbm,
    lim_hbm,
    u_hbm,
    p_hbm,
    x_out,
    u_out,
    p_out,
    w_out,
    cost,
    warm,
    xs,
    ss_row,
    st_row,
    load_ref,
    lim_ref,
    u_ref,
    p_ref,
    gs,
    zh,
    zl,
    hh,
    lb,
    at,
    oh,
    us,
    limtab,
    ptab,
    loadk,
    slot_of,
    u_fin,
    p_fin,
    wv,
    sb_l,
    rb_l,
    sb_r,
    rb_r,
    sb_x,
    rb_x,
    sb_o,
    rb_o,
    sb_s,
    rb_s,
    sb_q,
    rb_q,
    in_sem,
    out_sem,
    send_sem,
    l_sem,
    r_sem,
    x_sem,
    o_sem,
    s_sem,
    q_sem,
    p_sem,
):
    i, j = lax.axis_index("ship"), lax.axis_index("truck")
    c = lax.rem(i, NC)
    y = lax.rem(lax.div(i, NC), NY)
    x = lax.div(i, NC * NY)
    own = lax.rem(x + 2 * lax.rem(y, 2), NX) * NC + c
    row_scale = 1.0 / math.sqrt(TILE)
    cap_scale = 1.0 / math.sqrt(TILE * SHIP)

    def place(ox, oy, oc):
        px, py, pc = lax.rem(x + ox, NX), lax.rem(y + oy, NY), lax.rem(c + oc, NC)
        piece = lax.rem(px + 2 * lax.rem(py, 2), NX) * NC + pc
        return (px * NY + py) * NC + pc, piece

    cells = [(ox, oc) for ox in (2, 1, 3, 0) for oc in (1, 0)]
    takers = [
        (ox, oy, oc) for ox, oy in ((1, 0), (3, 0), (0, NY - 1), (0, 0)) for oc in (1, 0)
    ]

    def each_ship(act):
        def line(n, carry):
            half = (n + 1) // 2
            oy = jnp.where(n % 2 == 1, NY // 2 - half, NY // 2 + half)
            for ox, oc in cells:
                act(*place(ox, oy, oc))
            return carry

        lax.fori_loop(0, NY - 1, line, 0)
        for ox, oc in cells[:-1]:
            act(*place(ox, 0, oc))

    def z_at(n):
        half = (n + 1) // 2
        return lax.rem(j + jnp.where(n % 2 == 1, NZ // 2 - half, NZ // 2 + half), NZ)

    def each_truck(act):
        def line(n, carry):
            act(z_at(n))
            return carry

        lax.fori_loop(0, NZ - 1, line, 0)

    def each_taker(act):
        def line(n, carry):
            for at_offset in takers:
                act(place(*at_offset)[0], z_at(n))
            return carry

        lax.fori_loop(0, NZ - 1, line, 0)
        for at_offset in takers[:-1]:
            act(place(*at_offset)[0], j)

    barrier = pltpu.get_barrier_semaphore()

    def greet(di, dj):
        pl.semaphore_signal(barrier, inc=1, device_id=(di, dj), device_id_type=MESH)

    each_truck(lambda dj: greet(i, dj))
    each_ship(lambda di, d: greet(di, j))

    loads_in = [
        pltpu.make_async_copy(src, dst, in_sem.at[2, n])
        for n, (src, dst) in enumerate(
            (
                (ss_hbm, ss_row),
                (st_hbm, st_row),
                (load_hbm, load_ref),
                (lim_hbm, lim_ref),
                (u_hbm, u_ref),
                (p_hbm, p_ref),
            )
        )
    ]
    tiles_in = []
    for k in range(SLOTS):
        tiles_in += [
            pltpu.make_async_copy(warm_hbm.at[k], warm.at[k], in_sem.at[1, k]),
            pltpu.make_async_copy(cost_hbm.at[k], cost.at[k], in_sem.at[0, k]),
        ]
    for copy in loads_in + tiles_in:
        copy.start()

    def send(src, dst, sem, kind, it, di, dj):
        pltpu.make_async_remote_copy(
            src_ref=src,
            dst_ref=dst,
            send_sem=send_sem.at[kind, it],
            recv_sem=sem,
            device_id=(di, dj),
            device_id_type=MESH,
        ).start()

    def wait(buf, sem):
        pltpu.make_async_copy(buf, buf, sem).wait()

    for copy in loads_in:
        copy.wait()
    square = (SLOTS, SLOTS)
    diagonal = lax.broadcasted_iota(jnp.int32, square, 0) == lax.broadcasted_iota(
        jnp.int32, square, 1
    )

    def column(row):
        v = jnp.broadcast_to(row[...].astype(F32), square)
        return jnp.sum(jnp.where(diagonal, v, 0.0), axis=1, keepdims=True)

    ship_f = jnp.broadcast_to(column(ss_row), (SLOTS, TILE))
    ship_of = ship_f.astype(jnp.int32)
    truck_of = jnp.broadcast_to(column(st_row), (SLOTS, TILE)).astype(jnp.int32)
    slot_of[0] = ship_of
    slot_of[1] = truck_of
    sub = lax.broadcasted_iota(jnp.int32, (SLOTS, TILE), 0)
    for h in range(2):
        us[:, h * HALF : (h + 1) * HALF] = u_ref[pl.ds(h, SB, stride=2), :]
    for d in range(OWNERS):
        g, h = d // 2, d % 2
        for r in range(3):
            col = ((g % 2) * 3 + r) * TILE + h * HALF
            limtab[d, r : r + 1, :] = lim_ref[g // 2 : g // 2 + 1, col : col + HALF]
            ptab[0, d, r : r + 1, :] = p_ref[g // 2 : g // 2 + 1, col : col + HALF]
    for n in range(2):
        acc = jnp.zeros((SLOTS, TILE), F32)
        for s in range(SB):
            acc = jnp.where(
                ship_of == s, load_ref[n : n + 1, s * TILE : (s + 1) * TILE], acc
            )
        loadk[n] = acc
    for k in range(SLOTS):
        truck_k = jnp.broadcast_to(slot_of[1, k : k + 1, :], (SLOTS, TILE))
        hi, lo = [], []
        for g in range(4):
            v = jnp.broadcast_to(loadk[g // 2, k : k + 1, :], (SLOTS, TILE))
            v = jnp.where((sub < 3) & (truck_k == sub + 3 * (g % 2)), v, 0.0)
            a, b = split(v)
            hi.append(a)
            lo.append(b)
        lb[k] = jnp.concatenate(hi + lo, axis=0).astype(BF16)
    sb_o[...] = ship_f[:, :HALF]
    rb_o[j] = sb_o[...]
    one_row = lax.broadcasted_iota(jnp.int32, (16, TILE), 0)

    def prices_u():
        u8 = jnp.zeros((SLOTS, TILE), F32)
        for s in range(SB):
            u8 = jnp.where(ship_of == s, us[s : s + 1, :], u8)
        u_hi, u_lo = split(u8)
        a_hi, a_lo = split(loadk[0])
        b_hi, b_lo = split(loadk[1])
        stack = [u_hi, u_lo, a_hi, a_lo, a_hi, b_hi, b_lo, b_hi]
        stack.append(jnp.zeros((128 - 8 * len(stack), TILE), F32))
        at[...] = jnp.transpose(jnp.concatenate(stack, axis=0)).astype(BF16)

    def gradient(it):
        parts = []
        for n in range(2):
            p8 = []
            for h in range(2):
                acc = jnp.zeros((SLOTS, HALF), F32)
                for t in range(TB):
                    d = (2 * n + t // 3) * 2 + h
                    acc = jnp.where(
                        truck_of[:, :HALF] == t, ptab[it, d, t % 3 : t % 3 + 1, :], acc
                    )
                p8.append(acc)
            p_hi, p_lo = split(jnp.concatenate(p8, axis=1) * cap_scale)
            parts += [p_hi, p_hi, p_lo]
        ones = jnp.full((SLOTS, TILE), row_scale, F32)
        parts = [ones, ones] + parts
        for k in range(SLOTS):
            rows = [jnp.where(sub == k, v, 0.0) for v in parts]
            rows.append(jnp.zeros((128 - 8 * len(rows), TILE), F32))
            b_k = jnp.concatenate(rows, axis=0).astype(BF16)
            live = jnp.broadcast_to(slot_of[0, k : k + 1, :], (HALF, TILE)) >= 0
            for a in range(0, TILE, HALF):
                v = jnp.dot(at[a : a + HALF, :], b_k, preferred_element_type=F32)
                v = v + cost[k, a : a + HALF, :].astype(F32)
                gs[k, a : a + HALF, :] = jnp.where(live, v, 0.0)

    wv[...] = jnp.ones_like(wv)
    prices_u()
    for copy in tiles_in:
        copy.wait()
    for k in range(SLOTS):
        xs[k] = warm[k].astype(F32)
    gradient(0)

    pl.semaphore_wait(barrier, SHIP - 1 + NZ - 1)
    each_truck(lambda dj: send(sb_o, rb_o.at[j], o_sem.at[0], 4, 0, i, dj))

    def iteration(it, carry):
        weight = wv[...]
        tau = STEP / weight
        sigma = STEP * weight
        moved = jnp.zeros((8, HALF), F32)
        cap_hi = jnp.zeros((64, TILE), F32)
        cap_lo = jnp.zeros((32, TILE), F32)
        rows_acc = jnp.zeros((16, TILE), F32)
        nt = (((1,), (1,)), ((), ()))
        tau_b = jnp.broadcast_to(tau[0:1, 0:1], (ROWS, TILE))
        for k in range(SLOTS):
            for a in range(0, TILE, ROWS):
                old = xs[k, a : a + ROWS, :]
                new = jnp.clip(old - tau_b * gs[k, a : a + ROWS, :], 0.0, 1.0)
                xs[k, a : a + ROWS, :] = new
                step = new - old
                z = new + step
                z_hi = z.astype(BF16)
                zh[k, a : a + ROWS, :] = z_hi
                zl[k, a : a + ROWS, :] = (z - z_hi.astype(F32)).astype(BF16)
                zs = z[:, :HALF] + z[:, HALF:]
                s_hi = zs.astype(BF16)
                hh[k, a : a + ROWS, :HALF] = s_hi
                hh[k, a : a + ROWS, HALF:] = (zs - s_hi.astype(F32)).astype(BF16)
                sq = step * step
                sq = sq[:, :HALF] + sq[:, HALF:]
                moved = moved + jnp.sum(sq.reshape(ROWS // 8, 8, HALF), axis=0)
            if k == 0:
                continue
            pick = jnp.where(one_row == k - 1, 1.0, 0.0).astype(BF16)
            rows_acc = rows_acc + lax.dot_general(
                pick, hh[k - 1], nt, preferred_element_type=F32
            )
            cap_hi = cap_hi + jnp.dot(lb[k - 1], zh[k - 1], preferred_element_type=F32)
            cap_lo = cap_lo + jnp.dot(lb[k - 1, :32, :], zl[k - 1], preferred_element_type=F32)
        pick = jnp.where(one_row == SLOTS - 1, 1.0, 0.0).astype(BF16)
        rows_acc = rows_acc + lax.dot_general(
            pick, hh[SLOTS - 1], nt, preferred_element_type=F32
        )
        cap_hi = cap_hi + jnp.dot(lb[SLOTS - 1], zh[SLOTS - 1], preferred_element_type=F32)
        cap_lo = cap_lo + jnp.dot(lb[SLOTS - 1, :32, :], zl[SLOTS - 1], preferred_element_type=F32)
        sb_r[it] = rows_acc[:SLOTS]
        rb_r[it, j] = rows_acc[:SLOTS]
        each_truck(
            lambda dj: send(
                sb_r.at[it], rb_r.at[it, j], r_sem.at[it], 1, it, i, dj
            )
        )
        cap = cap_hi[:32] + cap_hi[32:] + cap_lo
        for d in range(OWNERS):
            g, h = d // 2, d % 2
            sb_l[it, d] = cap[8 * g : 8 * g + 3, h * HALF : (h + 1) * HALF]
        rb_l[it, i] = sb_l[it, own]
        each_ship(
            lambda di, d: send(
                sb_l.at[it, d], rb_l.at[it, i], l_sem.at[it], 0, it, di, j
            )
        )
        moved = jnp.sum(moved, axis=0, keepdims=True)
        sb_x[it] = moved
        rb_x[it, pl.ds(j, 1)] = moved
        each_truck(
            lambda dj: send(
                sb_x.at[it], rb_x.at[it, pl.ds(j, 1)], x_sem.at[it], 2, it, i, dj
            )
        )

        @pl.when(it == ITERS - 1)
        def _():
            pltpu.make_async_copy(xs, x_out, out_sem.at[0]).start()

        wait(rb_l.at[it, pl.ds(0, SHIP - 1)], l_sem.at[it])
        total = tree([rb_l[it, s] for s in range(SHIP)])
        old_p = ptab[it, own]
        sig3 = jnp.broadcast_to(sigma[0:1, 0:1], (3, HALF))
        new_p = jnp.maximum(
            old_p + sig3 * (cap_scale * total - cap_scale * limtab[own]), 0.0
        )
        ptab[it + 1, own] = new_p
        step_p = jnp.sum((new_p - old_p) ** 2, axis=0, keepdims=True)
        sb_s[it] = step_p
        rb_s[it, pl.ds(own * NZ + j, 1)] = step_p
        each_taker(
            lambda di, dj: send(
                sb_s.at[it], rb_s.at[it, pl.ds(own * NZ + j, 1)], s_sem.at[it], 3, it, di, dj
            )
        )
        for at_offset in takers[:-1]:
            send(
                ptab.at[it + 1, own],
                ptab.at[it + 1, own],
                p_sem.at[it],
                5,
                it,
                place(*at_offset)[0],
                j,
            )

        @pl.when(it == 0)
        def _():
            wait(rb_o.at[pl.ds(0, NZ - 1)], o_sem.at[0])
            lane = lax.broadcasted_iota(jnp.int32, (NZ * SLOTS, HALF), 1).astype(F32)
            hot = jnp.where(rb_o[...].reshape(NZ * SLOTS, HALF) == lane, 1.0, 0.0)
            hot = jnp.concatenate(
                [hot, jnp.zeros((128 - NZ * SLOTS, HALF), F32)], axis=0
            )
            hot = jnp.transpose(hot)[:32].astype(BF16)
            oh[...] = jnp.concatenate([hot, hot], axis=1)

        wait(rb_x.at[it, pl.ds(0, NZ - 1)], x_sem.at[it])
        step_x = jnp.sum(rb_x[it], axis=0, keepdims=True)
        step_x = step_x + pltpu.roll(step_x, HALF // 2, 1)
        wait(rb_r.at[it, pl.ds(0, NZ - 1)], r_sem.at[it])
        p_hi, p_lo = split(rb_r[it].reshape(NZ * SLOTS, TILE))
        gap = jnp.zeros((128 - NZ * SLOTS, TILE), F32)
        parts = jnp.concatenate([p_hi, gap, p_lo, gap], axis=0).astype(BF16)
        rows = jnp.dot(oh[...], parts, preferred_element_type=F32)
        rows = rows[:SB]
        old_u = us[...]
        sig24 = jnp.broadcast_to(sigma[0:1, 0:1], (SB, TILE))
        new_u = jnp.maximum(old_u + sig24 * (row_scale * rows - row_scale), 0.0)
        us[...] = new_u

        @pl.when(it == ITERS - 1)
        def _():
            for h in range(2):
                u_fin[pl.ds(h, SB, stride=2), :] = new_u[:, h * HALF : (h + 1) * HALF]
            pltpu.make_async_copy(u_fin, u_out, out_sem.at[1]).start()

        step_u = (new_u - old_u) ** 2
        step_u = jnp.sum(step_u[:, :HALF] + step_u[:, HALF:], axis=0, keepdims=True)
        step_u = step_u + pltpu.roll(step_u, HALF // 2, 1)
        low = lax.broadcasted_iota(jnp.int32, (1, HALF), 1) < HALF // 2
        both = jnp.where(low, step_x, step_u)
        sb_q[it] = both
        rb_q[it, pl.ds(i, 1)] = both
        each_ship(
            lambda di, d: send(
                sb_q.at[it], rb_q.at[it, pl.ds(i, 1)], q_sem.at[it], 6, it, di, j
            )
        )

        prices_u()
        wait(ptab.at[it + 1, pl.ds(0, OWNERS - 1)], p_sem.at[it])

        @pl.when(it == ITERS - 1)
        def _():
            for d in range(OWNERS):
                g, h = d // 2, d % 2
                for r in range(3):
                    col = ((g % 2) * 3 + r) * TILE + h * HALF
                    p_fin[g // 2 : g // 2 + 1, col : col + HALF] = ptab[
                        it + 1, d, r : r + 1, :
                    ]
            pltpu.make_async_copy(p_fin, p_out, out_sem.at[2]).start()

        gradient(it + 1)
        wait(rb_q.at[it, pl.ds(0, SHIP - 1)], q_sem.at[it])
        q_sum = jnp.sum(rb_q[it], axis=0, keepdims=True)
        wait(rb_s.at[it, pl.ds(0, OWNERS * NZ - 1)], s_sem.at[it])
        s_sum = jnp.sum(rb_s[it], axis=0, keepdims=True)
        dx = jnp.sum(jnp.where(low, q_sum, 0.0), axis=1, keepdims=True)
        dy = jnp.sum(jnp.where(low, 0.0, q_sum) + s_sum, axis=1, keepdims=True)
        weight = jnp.sqrt(
            weight[0:1, :]
            * jnp.sqrt(jnp.broadcast_to(dy, (1, HALF)) + EPS)
            / jnp.sqrt(jnp.broadcast_to(dx, (1, HALF)) + EPS)
        )
        wv[...] = jnp.broadcast_to(weight, wv.shape)
        return carry

    lax.fori_loop(0, ITERS, iteration, 0)

    w_out[...] = wv[0:1, :]
    for it in range(ITERS):
        wait(rb_l.at[it, pl.ds(0, SHIP - 1)], send_sem.at[0, it])
        wait(rb_r.at[it, pl.ds(0, NZ - 1)], send_sem.at[1, it])
        wait(rb_x.at[it, pl.ds(0, NZ - 1)], send_sem.at[2, it])
        wait(rb_s.at[it, pl.ds(0, OWNERS * NZ - 1)], send_sem.at[3, it])
        wait(ptab.at[it + 1, pl.ds(0, OWNERS - 1)], send_sem.at[5, it])
        wait(rb_q.at[it, pl.ds(0, SHIP - 1)], send_sem.at[6, it])
    wait(rb_o.at[pl.ds(0, NZ - 1)], send_sem.at[4, 0])
    pltpu.make_async_copy(xs, x_out, out_sem.at[0]).wait()
    pltpu.make_async_copy(u_fin, u_out, out_sem.at[1]).wait()
    pltpu.make_async_copy(p_fin, p_out, out_sem.at[2]).wait()


def copy_out(*refs):
    ins, outs, held, in_sem, out_sem = refs[:4], refs[4:8], refs[8:12], *refs[12:]
    pairs = [(ins[0].at[k], held[0].at[k], outs[0].at[k]) for k in range(SLOTS)]
    pairs += list(zip(ins[1:], held[1:], outs[1:]))
    first = [
        pltpu.make_async_copy(a, b, in_sem.at[n]) for n, (a, b, _) in enumerate(pairs)
    ]
    second = [
        pltpu.make_async_copy(b, c, out_sem.at[n]) for n, (_, b, c) in enumerate(pairs)
    ]
    for copy in first:
        copy.start()
    for a, b in zip(first, second):
        a.wait()
        b.start()
    for copy in second:
        copy.wait()


def on_device(cost, warm, slot_ship, slot_truck, load, limit, ship_price, truck_price):
    vmem, hbm = (
        pl.BlockSpec(memory_space=pltpu.VMEM),
        pl.BlockSpec(memory_space=pltpu.HBM),
    )
    dma = pltpu.SemaphoreType.DMA
    plan, prices, caps, weight = pl.pallas_call(
        kernel,
        out_shape=(
            jax.ShapeDtypeStruct((SLOTS, TILE, TILE), F32),
            jax.ShapeDtypeStruct((2 * SB, HALF), F32),
            jax.ShapeDtypeStruct(truck_price.shape, F32),
            jax.ShapeDtypeStruct((1, HALF), F32),
        ),
        in_specs=[hbm] * 8,
        out_specs=(hbm, hbm, hbm, vmem),
        scratch_shapes=[
            pltpu.VMEM((SLOTS, TILE, TILE), BF16),
            pltpu.VMEM((SLOTS, TILE, TILE), BF16),
            pltpu.VMEM((SLOTS, TILE, TILE), F32),
            pltpu.VMEM((1, SLOTS), jnp.int32),
            pltpu.VMEM((1, SLOTS), jnp.int32),
            pltpu.VMEM(load.shape, F32),
            pltpu.VMEM(limit.shape, F32),
            pltpu.VMEM((2 * SB, HALF), F32),
            pltpu.VMEM(truck_price.shape, F32),
            pltpu.VMEM((SLOTS, TILE, TILE), F32),
            pltpu.VMEM((SLOTS, TILE, TILE), BF16),
            pltpu.VMEM((SLOTS, TILE, TILE), BF16),
            pltpu.VMEM((SLOTS, TILE, TILE), BF16),
            pltpu.VMEM((SLOTS, 64, TILE), BF16),
            pltpu.VMEM((TILE, 128), BF16),
            pltpu.VMEM((32, 256), BF16),
            pltpu.VMEM((SB, TILE), F32),
            pltpu.VMEM((OWNERS, 3, HALF), F32),
            pltpu.VMEM((ITERS + 1, OWNERS, 3, HALF), F32),
            pltpu.VMEM((2, SLOTS, TILE), F32),
            pltpu.VMEM((2, SLOTS, TILE), jnp.int32),
            pltpu.VMEM((2 * SB, HALF), F32),
            pltpu.VMEM(truck_price.shape, F32),
            pltpu.VMEM((8, HALF), F32),
            pltpu.VMEM((ITERS, OWNERS, 3, HALF), F32),
            pltpu.VMEM((ITERS, SHIP, 3, HALF), F32),
            pltpu.VMEM((ITERS, SLOTS, TILE), F32),
            pltpu.VMEM((ITERS, NZ, SLOTS, TILE), F32),
            pltpu.VMEM((ITERS, 1, HALF), F32),
            pltpu.VMEM((ITERS, NZ, HALF), F32),
            pltpu.VMEM((SLOTS, HALF), F32),
            pltpu.VMEM((NZ, SLOTS, HALF), F32),
            pltpu.VMEM((ITERS, 1, HALF), F32),
            pltpu.VMEM((ITERS, OWNERS * NZ, HALF), F32),
            pltpu.VMEM((ITERS, 1, HALF), F32),
            pltpu.VMEM((ITERS, SHIP, HALF), F32),
            dma((3, SLOTS)),
            dma((3,)),
            dma((7, ITERS)),
            dma((ITERS,)),
            dma((ITERS,)),
            dma((ITERS,)),
            dma((1,)),
            dma((ITERS,)),
            dma((ITERS,)),
            dma((ITERS,)),
        ],
        compiler_params=pltpu.CompilerParams(
            collective_id=0, has_side_effects=True, vmem_limit_bytes=60 << 20
        ),
    )(
        cost.reshape(SLOTS, TILE, TILE),
        warm.reshape(SLOTS, TILE, TILE),
        slot_ship.reshape(1, SLOTS),
        slot_truck.reshape(1, SLOTS),
        load,
        limit,
        ship_price.reshape(2 * SB, HALF),
        truck_price,
    )
    results = (plan, prices, caps, weight)
    plan, prices, caps, weight = pl.pallas_call(
        copy_out,
        out_shape=[jax.ShapeDtypeStruct(v.shape, v.dtype) for v in results],
        in_specs=[hbm] * 4,
        out_specs=[hbm] * 4,
        scratch_shapes=[pltpu.VMEM(v.shape, v.dtype) for v in results]
        + [dma((SLOTS + 3,)), dma((SLOTS + 3,))],
    )(*results)
    return (
        plan.reshape(SLOTS, 1, TILE, TILE),
        prices.reshape(-1),
        caps,
        weight[0, 0],
    )


def solution(mesh):
    in_specs = (
        P("ship", "truck", None, None),
        P("ship", "truck", None, None),
        P("ship", "truck"),
        P("ship", "truck"),
        P(None, "ship"),
        P(None, "truck"),
        P("ship"),
        P(None, "truck"),
    )
    out_specs = (P("ship", "truck", None, None), P("ship"), P(None, "truck"), P())
    return jax.shard_map(
        on_device, mesh=mesh, in_specs=in_specs, out_specs=out_specs, check_vma=False
    )
```
